256 devices in a mesh: dp: 64 (over z, x, core), tensor: 4 (over y).
Axes of the slice: x: 4, y: 4, z: 8, core: 2. Of those that a mesh axis runs over, the one named last changes fastest.
Arguments:
- acts: bfloat16 [12288, 8192], P('dp', 'tensor'), may hold values from -6 to 6
- out_grads: bfloat16 [12288, 2, 28672], P('dp', None, 'tensor'), may hold values from -16 to 16
- projectors: bfloat16 [2, 8192, 64], replicated, may hold values from -0.75 to 0.75
- moment_first: float32 [28672, 128], P(('tensor', 'dp')), may hold values from -0.12 to 0.12
- moment_second: float32 [28672, 128], P(('tensor', 'dp')), may hold values from 1e-06 to 0.0001
Outputs:
- update: bfloat16 [2, 8192, 28672], P(None, 'dp', 'tensor')
- new_first: float32 [28672, 128], P(('tensor', 'dp'))
- new_second: float32 [28672, 128], P(('tensor', 'dp'))
The draws below stay inside these ranges and needn't reach their ends.
All inputs are finite; a program needn't handle non-finite values.
Results may differ from the reference program's by a relative error of at most 0.006.
Values may be sent and summed in bfloat16 or wider, within the bound.
A program may use at most 128 MiB of HBM per device.

```python
import math
import jax
import jax.numpy as jnp
from jax import lax

D = 8192
FF = 28672
R = 64
TOKENS = 12288
PAIR = 128


def spiked(entries, key, source, target, parts, factor):
    def block_of(position):
        return (jnp.arange(entries.shape[position]) // (entries.shape[position] // parts)).reshape((-1,) + (1,) * (entries.ndim - 1 - position))

    near = jax.random.permutation(key, parts)[block_of(target)]
    second = (block_of(target) + parts // 2) % parts
    return jnp.where((block_of(source) == near) | (block_of(source) == second), factor * entries, entries)


def block_scale(own_key, dims, cuts, least, largest):
    level, own = 1.0, jax.random.fold_in(own_key, 6)
    for position, blocks in cuts:
        draws = jnp.exp(jax.random.uniform(jax.random.fold_in(own, position), (blocks,), jnp.float32, least / len(cuts), largest / len(cuts)))
        level = level * jnp.repeat(draws, dims[position] // blocks).reshape([-1 if axis == position else 1 for axis in range(len(dims))])
    return level


def normal_values(stream_key, shape, spread, most, shards=(), held_as=jnp.bfloat16):
    result = jax.random.normal(stream_key, shape, jnp.float32) * spread
    if len(shards) > 0:
        result = block_scale(stream_key, shape, shards, -0.22, 0.18) * result
    return jnp.clip(result, min=-most, max=most).astype(held_as)


def gaussian_with(own_key, shape, width, reach, shards, heavy, dtype=jnp.bfloat16):
    entries = width * jax.random.normal(own_key, shape, jnp.float32)
    if shards:
        entries = entries * block_scale(own_key, shape, shards, -0.22, 0.18)
    return jnp.clip(spiked(entries, jax.random.fold_in(own_key, 3), *heavy), -reach, reach).astype(dtype)


def setup_inputs(seed: int = 0) -> dict:
    seeds = jax.random.split(jax.random.key(seed), 6)
    acts = normal_values(seeds[0], (TOKENS, D), 1.0, 6.0, ((0, 64), (1, 4)))
    out_grads = gaussian_with(seeds[1], (TOKENS, 2, FF), 1.0, 16.0, ((0, 64), (2, 4)), (0, 2, 64, 4.0))
    projectors = normal_values(seeds[2], (2, D, R), R ** -0.5, 0.75)
    moment_first = normal_values(seeds[3], (FF, PAIR), 0.02, 0.12, ((0, 256),), jnp.float32)
    moment_second = jnp.clip(jnp.exp(math.log(0.0001) - 4.6051702 * jax.random.uniform(seeds[4], (FF, PAIR), jnp.float32) ** block_scale(seeds[4], (FF, PAIR), ((0, 256),), -0.2, 0.2)), 9.999999974752427e-07, 0.0001)
    return {"acts": acts, "out_grads": out_grads, "projectors": projectors, "moment_first": moment_first, "moment_second": moment_second}


corr_one = 1.0 - 0.9 ** 10
corr_two = 1.0 - 0.999 ** 10

def reference(acts, out_grads, projectors, moment_first, moment_second):
    reduced = [jnp.dot(acts, projectors[k], preferred_element_type=jnp.float32).astype(jnp.bfloat16) for k in range(2)]
    pieces = []
    for k in range(2):
        part = lax.dot_general(out_grads[:, k, :], reduced[k], (((0,), (0,)), ((), ())), preferred_element_type=jnp.float32)
        pieces.append(part)
    grad = jnp.concatenate(pieces, axis=1) / jnp.float32(TOKENS)
    new_first = 0.9 * moment_first + 0.1 * grad
    new_second = 0.999 * moment_second + 0.001 * grad * grad
    normed = (new_first / corr_one / (jnp.sqrt(new_second / corr_two) + 1e-08)).astype(jnp.bfloat16)
    outs = []
    for k in range(2):
        block = normed[:, k * R:(k + 1) * R]
        outs.append(lax.dot_general(projectors[k], block, (((1,), (1,)), ((), ())), preferred_element_type=jnp.float32).astype(jnp.bfloat16))
    update = jnp.stack(outs, axis=0)
    return (update, new_first, new_second)
```

```python
import functools

import jax
import jax.numpy as jnp
from jax import lax
from jax.experimental import pallas as pl
from jax.experimental.pallas import tpu as pltpu
from jax.sharding import PartitionSpec as P

MESH = pl.DeviceIdType.MESH
corr_one = 1.0 - 0.9**10
corr_two = 1.0 - 0.999**10

NZ, NX, NC, NY = 8, 4, 2, 4
bf16, f32 = jnp.bfloat16, jnp.float32


def adam(grad, first, second):
    new_first = 0.9 * first + 0.1 * grad
    new_second = 0.999 * second + 0.001 * grad * grad
    return new_first, new_second


def normalize(new_first, new_second):
    return new_first / corr_one / (jnp.sqrt(new_second / corr_two) + 1e-08)


def reduce_gather(
    tokens, acts, proj, grads, first, second,
    gathered, grad_out,
    acts_v, proj_v, grads_v, first_v, second_v,
    xp_own, xp_in, part, part_send, core_in, x_send, x_in, z_send, z_own, z_in,
    in_sem, og_sem, y_s, y_r, c_s, c_r, x_s, x_r, z_s, z_r,
    gz_s, gz_r, gx_s, gx_r, gc_s, gc_r,
):
    t_count, _, columns = grads.shape
    group = columns // NZ
    own = group // (NX * NC)
    width = acts.shape[1]
    rank = proj.shape[1]
    pair = 2 * rank
    dp, y = lax.axis_index("dp"), lax.axis_index("tensor")
    z, x, c = dp // (NX * NC), lax.rem(dp // NC, NX), lax.rem(dp, NC)

    def zdev(j):
        return ((lax.rem(z + j, NZ) * NX + x) * NC + c, y)

    def xdev(j):
        return ((z * NX + lax.rem(x + j, NX)) * NC + c, y)

    def ydev(j):
        return (dp, lax.rem(y + j, NY))

    sibling = ((z * NX + x) * NC + (1 - c), y)

    def remote(src, dst, s, r, device):
        return pltpu.make_async_remote_copy(
            src_ref=src, dst_ref=dst, send_sem=s, recv_sem=r, device_id=device, device_id_type=MESH
        )

    load_acts = pltpu.make_async_copy(acts, acts_v, in_sem.at[0])
    load_proj = pltpu.make_async_copy(proj.at[:, :, pl.ds(pl.multiple_of(y * width, 128), width)], proj_v, in_sem.at[1])
    load_first = pltpu.make_async_copy(first, first_v, in_sem.at[2])
    load_second = pltpu.make_async_copy(second, second_v, in_sem.at[3])
    load_acts.start()
    load_proj.start()

    def offset(s):
        return NZ // 2 + (1 - 2 * lax.rem(s, 2)) * ((s + 1) // 2)

    def load_group(s):
        g = lax.rem(z + offset(s), NZ)
        span = pl.ds(pl.multiple_of(g * group, 128), group)
        return pltpu.make_async_copy(grads.at[:, :, span], grads_v.at[s], og_sem.at[s])

    @pl.loop(0, NZ)
    def _(s):
        load_group(s).start()

    load_first.start()
    load_second.start()

    barrier = pltpu.get_barrier_semaphore()
    peers = [zdev(j) for j in range(1, NZ)] + [xdev(j) for j in range(1, NX)] + [ydev(j) for j in range(1, NY)] + [sibling]
    for peer in peers:
        pl.semaphore_signal(barrier, inc=1, device_id=peer, device_id_type=MESH)

    load_acts.wait()
    load_proj.wait()
    nt = (((1,), (1,)), ((), ()))
    xp_own[...] = lax.dot_general(acts_v[...], proj_v[...].reshape(pair, width), nt, preferred_element_type=f32)
    pl.semaphore_wait(barrier, len(peers))

    y_copies = [remote(xp_own, xp_in.at[j - 1], y_s.at[j - 1], y_r.at[j - 1], ydev(j)) for j in range(1, NY)]
    for copy in y_copies:
        copy.start()
    row = lax.broadcasted_iota(jnp.int32, (2 * t_count, t_count), 0)
    col = lax.broadcasted_iota(jnp.int32, (2 * t_count, t_count), 1)
    spread = jnp.where(row // 2 == col, 1.0, 0.0).astype(bf16)
    for copy in y_copies:
        copy.wait_recv()
    reduced = (xp_own[...] + xp_in[0] + xp_in[1] + xp_in[2]).astype(bf16)
    weights = lax.dot_general(reduced, spread, (((0,), (1,)), ((), ())), preferred_element_type=f32)
    row = lax.broadcasted_iota(jnp.int32, (pair, 2 * t_count), 0)
    col = lax.broadcasted_iota(jnp.int32, (pair, 2 * t_count), 1)
    weights = jnp.where(lax.rem(col, 2) == row // rank, weights, 0.0).astype(bf16)

    def core_copy(s):
        return remote(part_send.at[s, :, 1 - c], core_in.at[s], c_s.at[s], c_r.at[s], sibling)

    def x_copy(s, j):
        return remote(x_send.at[s, lax.rem(x + j, NX)], x_in.at[s, j - 1], x_s.at[s, j - 1], x_r.at[s, j - 1], xdev(j))

    def z_copy(s):
        j = offset(s)
        return remote(z_send.at[s], z_in.at[s], z_s.at[s], z_r.at[s], zdev(j))

    lag = 2

    @pl.loop(0, NZ + lag)
    def _(step):
        @pl.when(step < NZ)
        def _():
            load_group(step).wait()
            block = grads_v[step].reshape(2 * t_count, group)
            terms = jnp.dot(weights, block, preferred_element_type=f32).T.reshape(NX, NC, own, pair)
            part[step] = terms
            part_send[step] = terms.astype(bf16)
            core_copy(step).start()

        @pl.when(step >= lag)
        def _():
            s = step - lag
            core_copy(s).wait_recv()
            x_send[s] = (part[s, :, c] + core_in[s].astype(f32)).astype(bf16)
            for j in (2, 1, 3):
                x_copy(s, j).start()

    def x_sum(s):
        for j in range(1, NX):
            x_copy(s, j).wait_recv()
        total = part[s, x, c] + core_in[s, x].astype(f32)
        for j in range(NX - 1):
            total += x_in[s, j].astype(f32)
        return total

    @pl.loop(0, NZ - 1)
    def _(s):
        z_send[s] = x_sum(s).astype(bf16)
        z_copy(s).start()

    total = x_sum(NZ - 1)
    for s in range(NZ - 1):
        z_copy(s).wait_recv()
        total += z_in[s].astype(f32)
    grad = total / f32(tokens)
    grad_out[...] = grad
    load_first.wait()
    load_second.wait()
    gathered[z, x, c] = normalize(*adam(grad, first_v[...], second_v[...])).astype(bf16)

    def gz_copy(j):
        here = gathered.at[z, x, c]
        return remote(here, here, gz_s.at[j - 1], gz_r.at[j - 1], zdev(j))

    def gz_arrival(j):
        here = gathered.at[lax.rem(z + NZ - j, NZ), x, c]
        return remote(here, here, gz_s.at[j - 1], gz_r.at[j - 1], zdev(j))

    def near(s):
        return offset(NZ - 1 - s)

    def gx_copy(s, j):
        here = gathered.at[lax.rem(z + NZ - near(s), NZ), x, c]
        return remote(here, here, gx_s.at[s, j - 1], gx_r.at[s, j - 1], xdev(j))

    def gx_arrival(s, j):
        here = gathered.at[lax.rem(z + NZ - near(s), NZ), lax.rem(x + NX - j, NX), c]
        return remote(here, here, gx_s.at[s, j - 1], gx_r.at[s, j - 1], xdev(j))

    def gc_copy(s, j):
        here = gathered.at[lax.rem(z + NZ - near(s), NZ), lax.rem(x + NX - j, NX), c]
        return remote(here, here, gc_s.at[s, j], gc_r.at[s, j], sibling)

    def gc_arrival(s, j):
        here = gathered.at[lax.rem(z + NZ - near(s), NZ), lax.rem(x + NX - j, NX), 1 - c]
        return remote(here, here, gc_s.at[s, j], gc_r.at[s, j], sibling)

    for j in (4, 3, 5, 2, 6, 1, 7):
        gz_copy(j).start()

    @pl.loop(0, NZ)
    def _(s):
        @pl.when(s > 0)
        def _():
            gz_arrival(near(s)).wait_recv()

        for j in (2, 1, 3):
            gx_copy(s, j).start()
        gc_copy(s, 0).start()

    @pl.loop(0, NZ)
    def _(s):
        for j in (1, 3, 2):
            gx_arrival(s, j).wait_recv()
            gc_copy(s, j).start()

    for copy in y_copies:
        copy.wait_send()
    for j in range(1, NZ):
        gz_copy(j).wait_send()

    @pl.loop(0, NZ)
    def _(s):
        core_copy(s).wait_send()
        for j in range(1, NX):
            x_copy(s, j).wait_send()

        @pl.when(s < NZ - 1)
        def _():
            z_copy(s).wait_send()

        for j in range(1, NX):
            gx_copy(s, j).wait_send()
        for j in range(NX):
            gc_copy(s, j).wait_send()
            gc_arrival(s, j).wait_recv()


def decode(normed, grad, first, second, proj, update, new_first, new_second, proj_v, out_v, in_sem, out_sem):
    columns = normed.shape[0]
    rank, rows = proj_v.shape[1], proj_v.shape[2]
    dp = lax.axis_index("dp")
    load = pltpu.make_async_copy(proj.at[:, :, pl.ds(pl.multiple_of(dp * rows, 128), rows)], proj_v, in_sem)
    load.start()
    new_first[...], new_second[...] = adam(grad[...], first[...], second[...])
    load.wait()
    flat = proj_v[...].reshape(2 * rank, rows)
    flat = jnp.concatenate([flat, flat], axis=1)
    row = lax.broadcasted_iota(jnp.int32, flat.shape, 0)
    col = lax.broadcasted_iota(jnp.int32, flat.shape, 1)
    flat = jnp.where(row // rank == col // rows, flat.astype(f32), 0.0).T.astype(bf16)
    chunk = columns // NZ

    def store(s):
        return pltpu.make_async_copy(out_v.at[s], update.at[:, :, pl.ds(pl.multiple_of(s * chunk, 128), chunk)], out_sem.at[s])

    @pl.loop(0, NZ)
    def _(s):
        block = normed[pl.ds(pl.multiple_of(s * chunk, 16), chunk), :]
        out = lax.dot_general(flat, block, (((1,), (1,)), ((), ())), preferred_element_type=f32)
        out_v[s] = out.astype(bf16).reshape(2, rows, chunk)
        store(s).start()

    @pl.loop(0, NZ)
    def _(s):
        store(s).wait()


def local(acts, out_grads, projectors, moment_first, moment_second):
    t_count, width = acts.shape
    columns = out_grads.shape[2]
    rank = projectors.shape[2]
    pair = 2 * rank
    dp_count = lax.axis_size("dp")
    own = columns // dp_count
    group = columns // NZ
    proj = jnp.swapaxes(projectors, 1, 2)
    hbm = pl.BlockSpec(memory_space=pl.ANY)
    vmem = pl.BlockSpec(memory_space=pltpu.VMEM)
    dma = pltpu.SemaphoreType.DMA
    gathered, grad = pl.pallas_call(
        functools.partial(reduce_gather, t_count * dp_count),
        out_shape=(
            jax.ShapeDtypeStruct((NZ, NX, NC, own, pair), bf16),
            jax.ShapeDtypeStruct((own, pair), f32),
        ),
        in_specs=[hbm] * 5,
        out_specs=(vmem, vmem),
        scratch_shapes=[
            pltpu.VMEM((t_count, width), bf16),
            pltpu.VMEM((2, rank, width), bf16),
            pltpu.VMEM((NZ, t_count, 2, group), bf16),
            pltpu.VMEM((own, pair), f32),
            pltpu.VMEM((own, pair), f32),
            pltpu.VMEM((t_count, pair), f32),
            pltpu.VMEM((NY - 1, t_count, pair), f32),
            pltpu.VMEM((NZ, NX, NC, own, pair), f32),
            pltpu.VMEM((NZ, NX, NC, own, pair), bf16),
            pltpu.VMEM((NZ, NX, own, pair), bf16),
            pltpu.VMEM((NZ, NX, own, pair), bf16),
            pltpu.VMEM((NZ, NX - 1, own, pair), bf16),
            pltpu.VMEM((NZ - 1, own, pair), bf16),
            pltpu.VMEM((own, pair), f32),
            pltpu.VMEM((NZ - 1, own, pair), bf16),
            dma((4,)),
            dma((NZ,)),
            dma((NY - 1,)),
            dma((NY - 1,)),
            dma((NZ,)),
            dma((NZ,)),
            dma((NZ, NX - 1)),
            dma((NZ, NX - 1)),
            dma((NZ - 1,)),
            dma((NZ - 1,)),
            dma((NZ - 1,)),
            dma((NZ - 1,)),
            dma((NZ, NX - 1)),
            dma((NZ, NX - 1)),
            dma((NZ, NX)),
            dma((NZ, NX)),
        ],
        compiler_params=pltpu.CompilerParams(collective_id=0, has_side_effects=True, vmem_limit_bytes=40 << 20),
        name="reduce_gather",
    )(acts, proj, out_grads, moment_first, moment_second)
    rows = projectors.shape[1] // dp_count
    return pl.pallas_call(
        decode,
        out_shape=(
            jax.ShapeDtypeStruct((2, rows, columns), bf16),
            jax.ShapeDtypeStruct(moment_first.shape, f32),
            jax.ShapeDtypeStruct(moment_second.shape, f32),
        ),
        in_specs=[vmem] * 4 + [hbm],
        out_specs=(hbm, vmem, vmem),
        scratch_shapes=[
            pltpu.VMEM((2, rank, rows), bf16),
            pltpu.VMEM((NZ, 2, rows, group), bf16),
            dma,
            dma((NZ,)),
        ],
        compiler_params=pltpu.CompilerParams(vmem_limit_bytes=40 << 20),
        name="decode",
    )(gathered.reshape(columns, pair), grad, moment_first, moment_second, proj)


def solution(mesh):
    return jax.shard_map(
        local,
        mesh=mesh,
        in_specs=(
            P("dp", "tensor"),
            P("dp", None, "tensor"),
            P(),
            P(("tensor", "dp"), None),
            P(("tensor", "dp"), None),
        ),
        out_specs=(P(None, "dp", "tensor"), P(("tensor", "dp"), None), P(("tensor", "dp"), None)),
        check_vma=False,
    )
```

```python
import functools

import jax
import jax.numpy as jnp
from jax import lax
from jax.experimental import pallas as pl
from jax.experimental.pallas import tpu as pltpu
from jax.sharding import PartitionSpec as P

MESH = pl.DeviceIdType.MESH
corr_one = 1.0 - 0.9**10
corr_two = 1.0 - 0.999**10

NZ, NX, NC, NY = 8, 4, 2, 4
bf16, f32 = jnp.bfloat16, jnp.float32


def adam(grad, first, second):
    new_first = 0.9 * first + 0.1 * grad
    new_second = 0.999 * second + 0.001 * grad * grad
    return new_first, new_second


def normalize(new_first, new_second):
    return new_first / corr_one / (jnp.sqrt(new_second / corr_two) + 1e-08)


def reduce_gather(
    tokens, acts, proj, grads, first, second,
    update, new_first, new_second,
    acts_v, proj_v, rows_v, grads_v, first_v, second_v,
    xp_own, xp_in, part, part_send, core_in, x_send, x_in, z_send, z_in, gathered,
    in_sem, og_sem, y_s, y_r, c_s, c_r, x_s, x_r, z_s, z_r,
    gz_s, gz_r, gx_s, gx_r, gc_s, gc_r,
):
    t_count, _, columns = grads.shape
    group = columns // NZ
    own = group // (NX * NC)
    width = acts.shape[1]
    rank = proj.shape[1]
    pair = 2 * rank
    dp, y = lax.axis_index("dp"), lax.axis_index("tensor")
    z, x, c = dp // (NX * NC), lax.rem(dp // NC, NX), lax.rem(dp, NC)

    def zdev(j):
        return ((lax.rem(z + j, NZ) * NX + x) * NC + c, y)

    def xdev(j):
        return ((z * NX + lax.rem(x + j, NX)) * NC + c, y)

    def ydev(j):
        return (dp, lax.rem(y + j, NY))

    sibling = ((z * NX + x) * NC + (1 - c), y)

    def remote(src, dst, s, r, device):
        return pltpu.make_async_remote_copy(
            src_ref=src, dst_ref=dst, send_sem=s, recv_sem=r, device_id=device, device_id_type=MESH
        )

    load_acts = pltpu.make_async_copy(acts, acts_v, in_sem.at[0])
    load_proj = pltpu.make_async_copy(proj.at[:, :, pl.ds(pl.multiple_of(y * width, 128), width)], proj_v, in_sem.at[1])
    load_first = pltpu.make_async_copy(first, first_v, in_sem.at[2])
    load_second = pltpu.make_async_copy(second, second_v, in_sem.at[3])
    rows = update.shape[1]
    load_rows = pltpu.make_async_copy(proj.at[:, :, pl.ds(pl.multiple_of(dp * rows, 128), rows)], rows_v, in_sem.at[4])
    load_acts.start()
    load_proj.start()
    load_rows.start()

    def offset(s):
        return NZ // 2 + (1 - 2 * lax.rem(s, 2)) * ((s + 1) // 2)

    def load_group(s):
        g = lax.rem(z + offset(s), NZ)
        span = pl.ds(pl.multiple_of(g * group, 128), group)
        return pltpu.make_async_copy(grads.at[:, :, span], grads_v.at[s], og_sem.at[s])

    barrier = pltpu.get_barrier_semaphore()
    peers = [zdev(j) for j in range(1, NZ)] + [xdev(j) for j in range(1, NX)] + [ydev(j) for j in range(1, NY)] + [sibling]
    for peer in peers:
        pl.semaphore_signal(barrier, inc=1, device_id=peer, device_id_type=MESH)

    load_acts.wait()
    load_proj.wait()

    @pl.loop(0, NZ)
    def _(s):
        load_group(s).start()

    load_first.start()
    load_second.start()

    nt = (((1,), (1,)), ((), ()))
    xp = lax.dot_general(acts_v[...], proj_v[...].reshape(pair, width), nt, preferred_element_type=f32)
    xp_own[...] = xp.astype(bf16)
    pl.semaphore_wait(barrier, len(peers))

    y_copies = [remote(xp_own, xp_in.at[j - 1], y_s.at[j - 1], y_r.at[j - 1], ydev(j)) for j in range(1, NY)]
    for j in (1, 0, 2):
        y_copies[j].start()
    row = lax.broadcasted_iota(jnp.int32, (t_count, 2 * t_count), 0)
    col = lax.broadcasted_iota(jnp.int32, (t_count, 2 * t_count), 1)
    spread = jnp.where(row == col // 2, 1.0, 0.0).astype(bf16)
    load_rows.wait()
    flat = rows_v[...].reshape(pair, rows)
    flat = jnp.concatenate([flat, flat], axis=1)
    row = lax.broadcasted_iota(jnp.int32, flat.shape, 0)
    col = lax.broadcasted_iota(jnp.int32, flat.shape, 1)
    decoder = jnp.where(row // rank == col // rows, flat.astype(f32), 0.0).T.astype(bf16)
    for copy in y_copies:
        copy.wait_recv()
    reduced = (xp + xp_in[0].astype(f32) + xp_in[1].astype(f32) + xp_in[2].astype(f32)).astype(bf16)
    weights = jnp.dot(reduced.T, spread, preferred_element_type=f32)
    row = lax.broadcasted_iota(jnp.int32, (pair, 2 * t_count), 0)
    col = lax.broadcasted_iota(jnp.int32, (pair, 2 * t_count), 1)
    weights = jnp.where(lax.rem(col, 2) == row // rank, weights, 0.0).astype(bf16)

    def core_copy(s):
        return remote(part_send.at[s, :, 1 - c], core_in.at[s], c_s.at[s], c_r.at[s], sibling)

    def x_copy(s, j):
        return remote(x_send.at[s, lax.rem(x + j, NX)], x_in.at[s, j - 1], x_s.at[s, j - 1], x_r.at[s, j - 1], xdev(j))

    def z_copy(s):
        j = offset(s)
        return remote(z_send.at[s], z_in.at[s], z_s.at[s], z_r.at[s], zdev(j))

    lag = 4

    @pl.loop(0, NZ + lag)
    def _(step):
        @pl.when(step < NZ)
        def _():
            load_group(step).wait()
            block = grads_v[step].reshape(2 * t_count, group)
            terms = jnp.dot(weights, block, preferred_element_type=f32).T.reshape(NX, NC, own, pair)
            part[step] = terms
            part_send[step] = terms.astype(bf16)
            core_copy(step).start()

        @pl.when(step >= lag)
        def _():
            s = step - lag
            core_copy(s).wait_recv()
            x_send[s] = (part[s, :, c] + core_in[s].astype(f32)).astype(bf16)
            for j in (2, 1, 3):
                x_copy(s, j).start()

    def x_sum(s):
        for j in range(1, NX):
            x_copy(s, j).wait_recv()
        total = part[s, x, c] + core_in[s, x].astype(f32)
        for j in range(NX - 1):
            total += x_in[s, j].astype(f32)
        return total

    @pl.loop(0, NZ - 1)
    def _(s):
        z_send[s] = x_sum(s).astype(bf16)
        z_copy(s).start()

    total = x_sum(NZ - 1)
    for s in range(NZ - 1):
        z_copy(s).wait_recv()
        total += z_in[s].astype(f32)
    grad = total / f32(tokens)
    load_first.wait()
    load_second.wait()
    new_first[...], new_second[...] = adam(grad, first_v[...], second_v[...])
    gathered[z, x, c] = normalize(new_first[...], new_second[...]).astype(bf16)

    def gz_copy(j):
        here = gathered.at[z, x, c]
        return remote(here, here, gz_s.at[j - 1], gz_r.at[j - 1], zdev(j))

    def gz_arrival(j):
        here = gathered.at[lax.rem(z + NZ - j, NZ), x, c]
        return remote(here, here, gz_s.at[j - 1], gz_r.at[j - 1], zdev(j))

    def near(s):
        return offset(NZ - 1 - s)

    def gx_copy(s, j):
        here = gathered.at[lax.rem(z + NZ - near(s), NZ), x, c]
        return remote(here, here, gx_s.at[s, j - 1], gx_r.at[s, j - 1], xdev(j))

    def gx_arrival(s, j):
        here = gathered.at[lax.rem(z + NZ - near(s), NZ), lax.rem(x + NX - j, NX), c]
        return remote(here, here, gx_s.at[s, j - 1], gx_r.at[s, j - 1], xdev(j))

    def gc_copy(s):
        here = gathered.at[lax.rem(z + NZ - near(s), NZ), :, c]
        return remote(here, here, gc_s.at[s], gc_r.at[s], sibling)

    def gc_arrival(s):
        here = gathered.at[lax.rem(z + NZ - near(s), NZ), :, 1 - c]
        return remote(here, here, gc_s.at[s], gc_r.at[s], sibling)

    for j in (1, 7, 2, 6, 3, 5, 4):
        gz_copy(j).start()

    x_lag, core_lag = 6, 8

    @pl.loop(0, NZ + core_lag)
    def _(step):
        @pl.when(step < NZ)
        def _():
            @pl.when(step > 0)
            def _():
                gz_arrival(near(step)).wait_recv()

            for j in (2, 1, 3):
                gx_copy(step, j).start()

        @pl.when((step >= x_lag) & (step < NZ + x_lag))
        def _():
            s = step - x_lag
            for j in range(1, NX):
                gx_arrival(s, j).wait_recv()
            gc_copy(s).start()

        @pl.when(step >= core_lag)
        def _():
            s = step - core_lag
            gc_arrival(s).wait_recv()
            g = lax.rem(z + NZ - near(s), NZ)
            block = gathered[g].reshape(group, pair)
            out = lax.dot_general(decoder, block, nt, preferred_element_type=f32)
            update[:, :, pl.ds(pl.multiple_of(g * group, 128), group)] = out.astype(bf16).reshape(2, rows, group)

    for copy in y_copies:
        copy.wait_send()
    for j in range(1, NZ):
        gz_copy(j).wait_send()

    @pl.loop(0, NZ)
    def _(s):
        core_copy(s).wait_send()
        for j in range(1, NX):
            x_copy(s, j).wait_send()

        @pl.when(s < NZ - 1)
        def _():
            z_copy(s).wait_send()

        for j in range(1, NX):
            gx_copy(s, j).wait_send()
        gc_copy(s).wait_send()


def publish(update, first, second, update_out, first_out, second_out, sem):
    pieces = update.shape[1] // 4
    copies = [
        pltpu.make_async_copy(update.at[:, pl.ds(i * pieces, pieces)], update_out.at[:, pl.ds(i * pieces, pieces)], sem.at[i])
        for i in range(4)
    ]
    copies.append(pltpu.make_async_copy(first, first_out, sem.at[4]))
    copies.append(pltpu.make_async_copy(second, second_out, sem.at[5]))
    for copy in copies:
        copy.start()
    for copy in copies:
        copy.wait()


def local(acts, out_grads, projectors, moment_first, moment_second):
    t_count, width = acts.shape
    columns = out_grads.shape[2]
    rank = projectors.shape[2]
    pair = 2 * rank
    dp_count = lax.axis_size("dp")
    own = columns // dp_count
    group = columns // NZ
    proj = jnp.swapaxes(projectors, 1, 2)
    rows = projectors.shape[1] // dp_count
    inputs = [pltpu.with_memory_space_constraint(a, pltpu.HBM) for a in (acts, proj, out_grads, moment_first, moment_second)]
    hbm = pl.BlockSpec(memory_space=pltpu.HBM)
    vmem = pl.BlockSpec(memory_space=pltpu.VMEM)
    dma = pltpu.SemaphoreType.DMA
    results = pl.pallas_call(
        functools.partial(reduce_gather, t_count * dp_count),
        out_shape=(
            pltpu.VMEM((2, rows, columns), bf16),
            pltpu.VMEM((own, pair), f32),
            pltpu.VMEM((own, pair), f32),
        ),
        in_specs=[hbm] * 5,
        out_specs=(vmem, vmem, vmem),
        scratch_shapes=[
            pltpu.VMEM((t_count, width), bf16),
            pltpu.VMEM((2, rank, width), bf16),
            pltpu.VMEM((2, rank, rows), bf16),
            pltpu.VMEM((NZ, t_count, 2, group), bf16),
            pltpu.VMEM((own, pair), f32),
            pltpu.VMEM((own, pair), f32),
            pltpu.VMEM((t_count, pair), bf16),
            pltpu.VMEM((NY - 1, t_count, pair), bf16),
            pltpu.VMEM((NZ, NX, NC, own, pair), f32),
            pltpu.VMEM((NZ, NX, NC, own, pair), bf16),
            pltpu.VMEM((NZ, NX, own, pair), bf16),
            pltpu.VMEM((NZ, NX, own, pair), bf16),
            pltpu.VMEM((NZ, NX - 1, own, pair), bf16),
            pltpu.VMEM((NZ - 1, own, pair), bf16),
            pltpu.VMEM((NZ - 1, own, pair), bf16),
            pltpu.VMEM((NZ, NX, NC, own, pair), bf16),
            dma((5,)),
            dma((NZ,)),
            dma((NY - 1,)),
            dma((NY - 1,)),
            dma((NZ,)),
            dma((NZ,)),
            dma((NZ, NX - 1)),
            dma((NZ, NX - 1)),
            dma((NZ - 1,)),
            dma((NZ - 1,)),
            dma((NZ - 1,)),
            dma((NZ - 1,)),
            dma((NZ, NX - 1)),
            dma((NZ, NX - 1)),
            dma((NZ,)),
            dma((NZ,)),
        ],
        compiler_params=pltpu.CompilerParams(collective_id=0, has_side_effects=True, vmem_limit_bytes=40 << 20),
        name="rank_adam",
    )(*inputs)
    return pl.pallas_call(
        publish,
        out_shape=tuple(jax.ShapeDtypeStruct(r.shape, r.dtype) for r in results),
        in_specs=[vmem] * 3,
        out_specs=[hbm] * 3,
        scratch_shapes=[dma((6,))],
        compiler_params=pltpu.CompilerParams(vmem_limit_bytes=4 << 20),
        name="publish",
    )(*[pltpu.with_memory_space_constraint(r, pltpu.VMEM) for r in results])


def solution(mesh):
    return jax.shard_map(
        local,
        mesh=mesh,
        in_specs=(
            P("dp", "tensor"),
            P("dp", None, "tensor"),
            P(),
            P(("tensor", "dp"), None),
            P(("tensor", "dp"), None),
        ),
        out_specs=(P(None, "dp", "tensor"), P(("tensor", "dp"), None), P(("tensor", "dp"), None)),
        check_vma=False,
    )
```

```python
import functools

import jax
import jax.numpy as jnp
from jax import lax
from jax.experimental import pallas as pl
from jax.experimental.pallas import tpu as pltpu
from jax.sharding import PartitionSpec as P

MESH = pl.DeviceIdType.MESH
corr_one = 1.0 - 0.9**10
corr_two = 1.0 - 0.999**10

HEAD = 80
NZ, NX, NC, NY = 8, 4, 2, 4
bf16, f32 = jnp.bfloat16, jnp.float32


def adam(grad, first, second):
    new_first = 0.9 * first + 0.1 * grad
    new_second = 0.999 * second + 0.001 * grad * grad
    return new_first, new_second


def normalize(new_first, new_second):
    return new_first / corr_one / (jnp.sqrt(new_second / corr_two) + 1e-08)


def reduce_gather(
    tokens, acts, proj, grads, first, second,
    update, new_first, new_second,
    acts_v, proj_v, rows_v, grads_v, first_v, second_v,
    xp_own, xp_in, part, part_send, core_in, x_send, x_in, z_send, z_in, tail_zin, tail_own, tail_send, tail_xin, gathered,
    in_sem, og_sem, y_s, y_r, c_s, c_r, x_s, x_r, z_s, z_r,
    gz_s, gz_r, gx_s, gx_r, gc_s, gc_r,
    tz_s, tz_r, tx_s, tx_r, gtz_s, gtz_r, gtx_s, gtx_r,
):
    t_count, _, columns = grads.shape
    group = columns // NZ
    own = group // (NX * NC)
    width = acts.shape[1]
    rank = proj.shape[1]
    pair = 2 * rank
    dp, y = lax.axis_index("dp"), lax.axis_index("tensor")
    z, x, c = dp // (NX * NC), lax.rem(dp // NC, NX), lax.rem(dp, NC)

    def zdev(j):
        return ((lax.rem(z + j, NZ) * NX + x) * NC + c, y)

    def xdev(j):
        return ((z * NX + lax.rem(x + j, NX)) * NC + c, y)

    def ydev(j):
        return (dp, lax.rem(y + j, NY))

    head, tail = pl.ds(0, HEAD), pl.ds(HEAD, own - HEAD)
    sibling = ((z * NX + x) * NC + (1 - c), y)

    def remote(src, dst, s, r, device):
        return pltpu.make_async_remote_copy(
            src_ref=src, dst_ref=dst, send_sem=s, recv_sem=r, device_id=device, device_id_type=MESH
        )

    load_acts = pltpu.make_async_copy(acts, acts_v, in_sem.at[0])
    load_proj = pltpu.make_async_copy(proj.at[:, :, pl.ds(pl.multiple_of(y * width, 128), width)], proj_v, in_sem.at[1])
    load_first = pltpu.make_async_copy(first, first_v, in_sem.at[2])
    load_second = pltpu.make_async_copy(second, second_v, in_sem.at[3])
    rows = update.shape[1]
    load_rows = pltpu.make_async_copy(proj.at[:, :, pl.ds(pl.multiple_of(dp * rows, 128), rows)], rows_v, in_sem.at[4])
    load_acts.start()
    load_proj.start()
    load_rows.start()

    def offset(s):
        return NZ // 2 + (1 - 2 * lax.rem(s, 2)) * ((s + 1) // 2)

    def load_group(s):
        g = lax.rem(z + offset(s), NZ)
        span = pl.ds(pl.multiple_of(g * group, 128), group)
        return pltpu.make_async_copy(grads.at[:, :, span], grads_v.at[s], og_sem.at[s])

    barrier = pltpu.get_barrier_semaphore()
    peers = [zdev(j) for j in range(1, NZ)] + [xdev(j) for j in range(1, NX)] + [ydev(j) for j in range(1, NY)] + [sibling]
    for peer in peers:
        pl.semaphore_signal(barrier, inc=1, device_id=peer, device_id_type=MESH)

    load_acts.wait()
    load_proj.wait()

    @pl.loop(0, NZ)
    def _(s):
        load_group(s).start()

    load_first.start()
    load_second.start()

    nt = (((1,), (1,)), ((), ()))
    xp = lax.dot_general(acts_v[...], proj_v[...].reshape(pair, width), nt, preferred_element_type=f32)
    xp_own[...] = xp.astype(bf16)
    pl.semaphore_wait(barrier, len(peers))

    y_copies = [remote(xp_own, xp_in.at[j - 1], y_s.at[j - 1], y_r.at[j - 1], ydev(j)) for j in range(1, NY)]
    for j in (1, 0, 2):
        y_copies[j].start()
    row = lax.broadcasted_iota(jnp.int32, (t_count, 2 * t_count), 0)
    col = lax.broadcasted_iota(jnp.int32, (t_count, 2 * t_count), 1)
    spread = jnp.where(row == col // 2, 1.0, 0.0).astype(bf16)
    load_rows.wait()
    flat = rows_v[...].reshape(pair, rows)
    flat = jnp.concatenate([flat, flat], axis=1)
    row = lax.broadcasted_iota(jnp.int32, flat.shape, 0)
    col = lax.broadcasted_iota(jnp.int32, flat.shape, 1)
    decoder = jnp.where(row // rank == col // rows, flat.astype(f32), 0.0).T.astype(bf16)
    for copy in y_copies:
        copy.wait_recv()
    reduced = (xp + xp_in[0].astype(f32) + xp_in[1].astype(f32) + xp_in[2].astype(f32)).astype(bf16)
    weights = jnp.dot(reduced.T, spread, preferred_element_type=f32)
    row = lax.broadcasted_iota(jnp.int32, (pair, 2 * t_count), 0)
    col = lax.broadcasted_iota(jnp.int32, (pair, 2 * t_count), 1)
    weights = jnp.where(lax.rem(col, 2) == row // rank, weights, 0.0).astype(bf16)

    def core_copy(s):
        return remote(part_send.at[s, :, 1 - c], core_in.at[s], c_s.at[s], c_r.at[s], sibling)

    def x_copy(s, j):
        return remote(x_send.at[s, lax.rem(x + j, NX), head], x_in.at[s, j - 1], x_s.at[s, j - 1], x_r.at[s, j - 1], xdev(j))

    def z_copy(s):
        j = offset(s)
        return remote(z_send.at[s], z_in.at[s], z_s.at[s], z_r.at[s], zdev(j))

    def tz_copy(s):
        return remote(x_send.at[s, :, tail], tail_zin.at[s], tz_s.at[s], tz_r.at[s], zdev(offset(s)))

    def tx_copy(j):
        return remote(tail_send.at[lax.rem(x + j, NX)], tail_xin.at[j - 1], tx_s.at[j - 1], tx_r.at[j - 1], xdev(j))

    lag = 4

    @pl.loop(0, NZ + lag)
    def _(step):
        @pl.when(step < NZ)
        def _():
            load_group(step).wait()
            block = grads_v[step].reshape(2 * t_count, group)
            terms = jnp.dot(weights, block, preferred_element_type=f32).T.reshape(NX, NC, own, pair)
            part[step] = terms
            part_send[step] = terms.astype(bf16)
            core_copy(step).start()

        @pl.when(step >= lag)
        def _():
            s = step - lag
            core_copy(s).wait_recv()
            x_send[s] = (part[s, :, c] + core_in[s].astype(f32)).astype(bf16)
            for j in (2, 1, 3):
                x_copy(s, j).start()

            @pl.when(s < NZ - 1)
            def _():
                tz_copy(s).start()

    def x_sum(s):
        for j in range(1, NX):
            x_copy(s, j).wait_recv()
        total = part[s, x, c, head] + core_in[s, x, head].astype(f32)
        for j in range(NX - 1):
            total += x_in[s, j].astype(f32)
        return total

    def x_then_z(s):
        z_send[s] = x_sum(s).astype(bf16)
        z_copy(s).start()

    pl.loop(0, 4)(x_then_z)
    tails = part[NZ - 1, :, c, tail] + core_in[NZ - 1, :, tail].astype(f32)
    for s in range(NZ - 1):
        tz_copy(s).wait_recv()
        tails += tail_zin[s].astype(f32)
    tail_send[...] = tails.astype(bf16)
    tail_own[...] = tails
    for j in (2, 1, 3):
        tx_copy(j).start()
    pl.loop(4, NZ - 1)(x_then_z)

    load_first.wait()
    load_second.wait()

    def finish(span, total):
        grad = total / f32(tokens)
        new_first[span], new_second[span] = adam(grad, first_v[span], second_v[span])
        gathered[z, x, c, span] = normalize(new_first[span], new_second[span]).astype(bf16)

    total = tail_own[x]
    for j in range(1, NX):
        tx_copy(j).wait_recv()
        total += tail_xin[j - 1].astype(f32)
    finish(tail, total)
    total = x_sum(NZ - 1)
    for s in range(NZ - 1):
        z_copy(s).wait_recv()
        total += z_in[s].astype(f32)
    finish(head, total)

    def gz_copy(j):
        here = gathered.at[z, x, c, head]
        return remote(here, here, gz_s.at[j - 1], gz_r.at[j - 1], zdev(j))

    def gz_arrival(j):
        here = gathered.at[lax.rem(z + NZ - j, NZ), x, c, head]
        return remote(here, here, gz_s.at[j - 1], gz_r.at[j - 1], zdev(j))

    def near(s):
        return offset(NZ - 1 - s)

    def gx_copy(s, j):
        here = gathered.at[lax.rem(z + NZ - near(s), NZ), x, c, head]
        return remote(here, here, gx_s.at[s, j - 1], gx_r.at[s, j - 1], xdev(j))

    def gx_arrival(s, j):
        here = gathered.at[lax.rem(z + NZ - near(s), NZ), lax.rem(x + NX - j, NX), c, head]
        return remote(here, here, gx_s.at[s, j - 1], gx_r.at[s, j - 1], xdev(j))

    def gtx_copy(j):
        here = gathered.at[z, x, c, tail]
        return remote(here, here, gtx_s.at[j - 1], gtx_r.at[j - 1], xdev(j))

    def gtx_arrival(j):
        here = gathered.at[z, lax.rem(x + NX - j, NX), c, tail]
        return remote(here, here, gtx_s.at[j - 1], gtx_r.at[j - 1], xdev(j))

    def gtz_copy(j):
        here = gathered.at[z, :, c, tail]
        return remote(here, here, gtz_s.at[j - 1], gtz_r.at[j - 1], zdev(j))

    def gtz_arrival(j):
        here = gathered.at[lax.rem(z + NZ - j, NZ), :, c, tail]
        return remote(here, here, gtz_s.at[j - 1], gtz_r.at[j - 1], zdev(j))

    def gc_copy(s):
        here = gathered.at[lax.rem(z + NZ - near(s), NZ), :, c]
        return remote(here, here, gc_s.at[s], gc_r.at[s], sibling)

    def gc_arrival(s):
        here = gathered.at[lax.rem(z + NZ - near(s), NZ), :, 1 - c]
        return remote(here, here, gc_s.at[s], gc_r.at[s], sibling)

    for j in (2, 1, 3):
        gtx_copy(j).start()
    for j in (1, 7, 2, 6, 3, 5, 4):
        gz_copy(j).start()

    x_lag, core_lag = 6, 8

    @pl.loop(0, NZ + core_lag)
    def _(step):
        @pl.when(step < NZ)
        def _():
            @pl.when(step > 0)
            def _():
                gz_arrival(near(step)).wait_recv()

            for j in (2, 1, 3):
                gx_copy(step, j).start()

        @pl.when(step == 1)
        def _():
            for j in range(1, NX):
                gtx_arrival(j).wait_recv()
            for j in (1, 7, 2, 6, 3, 5, 4):
                gtz_copy(j).start()

        @pl.when((step >= x_lag) & (step < NZ + x_lag))
        def _():
            s = step - x_lag
            for j in range(1, NX):
                gx_arrival(s, j).wait_recv()

            @pl.when(s > 0)
            def _():
                gtz_arrival(near(s)).wait_recv()

            gc_copy(s).start()

        @pl.when(step >= core_lag)
        def _():
            s = step - core_lag
            gc_arrival(s).wait_recv()
            g = lax.rem(z + NZ - near(s), NZ)
            block = gathered[g].reshape(group, pair)
            out = lax.dot_general(decoder, block, nt, preferred_element_type=f32)
            update[:, :, pl.ds(pl.multiple_of(g * group, 128), group)] = out.astype(bf16).reshape(2, rows, group)

    for copy in y_copies:
        copy.wait_send()
    for j in range(1, NZ):
        gz_copy(j).wait_send()
        gtz_copy(j).wait_send()
        tz_copy(j - 1).wait_send()
    for j in range(1, NX):
        tx_copy(j).wait_send()
        gtx_copy(j).wait_send()

    @pl.loop(0, NZ)
    def _(s):
        core_copy(s).wait_send()
        for j in range(1, NX):
            x_copy(s, j).wait_send()

        @pl.when(s < NZ - 1)
        def _():
            z_copy(s).wait_send()

        for j in range(1, NX):
            gx_copy(s, j).wait_send()
        gc_copy(s).wait_send()


def publish(update, first, second, update_out, first_out, second_out, sem):
    pieces = update.shape[1] // 4
    copies = [
        pltpu.make_async_copy(update.at[:, pl.ds(i * pieces, pieces)], update_out.at[:, pl.ds(i * pieces, pieces)], sem.at[i])
        for i in range(4)
    ]
    copies.append(pltpu.make_async_copy(first, first_out, sem.at[4]))
    copies.append(pltpu.make_async_copy(second, second_out, sem.at[5]))
    for copy in copies:
        copy.start()
    for copy in copies:
        copy.wait()


def local(acts, out_grads, projectors, moment_first, moment_second):
    t_count, width = acts.shape
    columns = out_grads.shape[2]
    rank = projectors.shape[2]
    pair = 2 * rank
    dp_count = lax.axis_size("dp")
    own = columns // dp_count
    group = columns // NZ
    proj = jnp.swapaxes(projectors, 1, 2)
    rows = projectors.shape[1] // dp_count
    inputs = [pltpu.with_memory_space_constraint(a, pltpu.HBM) for a in (acts, proj, out_grads, moment_first, moment_second)]
    hbm = pl.BlockSpec(memory_space=pltpu.HBM)
    vmem = pl.BlockSpec(memory_space=pltpu.VMEM)
    dma = pltpu.SemaphoreType.DMA
    results = pl.pallas_call(
        functools.partial(reduce_gather, t_count * dp_count),
        out_shape=(
            pltpu.VMEM((2, rows, columns), bf16),
            pltpu.VMEM((own, pair), f32),
            pltpu.VMEM((own, pair), f32),
        ),
        in_specs=[hbm] * 5,
        out_specs=(vmem, vmem, vmem),
        scratch_shapes=[
            pltpu.VMEM((t_count, width), bf16),
            pltpu.VMEM((2, rank, width), bf16),
            pltpu.VMEM((2, rank, rows), bf16),
            pltpu.VMEM((NZ, t_count, 2, group), bf16),
            pltpu.VMEM((own, pair), f32),
            pltpu.VMEM((own, pair), f32),
            pltpu.VMEM((t_count, pair), bf16),
            pltpu.VMEM((NY - 1, t_count, pair), bf16),
            pltpu.VMEM((NZ, NX, NC, own, pair), f32),
            pltpu.VMEM((NZ, NX, NC, own, pair), bf16),
            pltpu.VMEM((NZ, NX, own, pair), bf16),
            pltpu.VMEM((NZ, NX, own, pair), bf16),
            pltpu.VMEM((NZ, NX - 1, HEAD, pair), bf16),
            pltpu.VMEM((NZ - 1, HEAD, pair), bf16),
            pltpu.VMEM((NZ - 1, HEAD, pair), bf16),
            pltpu.VMEM((NZ - 1, NX, own - HEAD, pair), bf16),
            pltpu.VMEM((NX, own - HEAD, pair), f32),
            pltpu.VMEM((NX, own - HEAD, pair), bf16),
            pltpu.VMEM((NX - 1, own - HEAD, pair), bf16),
            pltpu.VMEM((NZ, NX, NC, own, pair), bf16),
            dma((5,)),
            dma((NZ,)),
            dma((NY - 1,)),
            dma((NY - 1,)),
            dma((NZ,)),
            dma((NZ,)),
            dma((NZ, NX - 1)),
            dma((NZ, NX - 1)),
            dma((NZ - 1,)),
            dma((NZ - 1,)),
            dma((NZ - 1,)),
            dma((NZ - 1,)),
            dma((NZ, NX - 1)),
            dma((NZ, NX - 1)),
            dma((NZ,)),
            dma((NZ,)),
            dma((NZ - 1,)),
            dma((NZ - 1,)),
            dma((NX - 1,)),
            dma((NX - 1,)),
            dma((NZ - 1,)),
            dma((NZ - 1,)),
            dma((NX - 1,)),
            dma((NX - 1,)),
        ],
        compiler_params=pltpu.CompilerParams(collective_id=0, has_side_effects=True, vmem_limit_bytes=40 << 20),
        name="rank_adam",
    )(*inputs)
    return pl.pallas_call(
        publish,
        out_shape=tuple(jax.ShapeDtypeStruct(r.shape, r.dtype) for r in results),
        in_specs=[vmem] * 3,
        out_specs=[hbm] * 3,
        scratch_shapes=[dma((6,))],
        compiler_params=pltpu.CompilerParams(vmem_limit_bytes=4 << 20),
        name="publish",
    )(*[pltpu.with_memory_space_constraint(r, pltpu.VMEM) for r in results])


def solution(mesh):
    return jax.shard_map(
        local,
        mesh=mesh,
        in_specs=(
            P("dp", "tensor"),
            P("dp", None, "tensor"),
            P(),
            P(("tensor", "dp"), None),
            P(("tensor", "dp"), None),
        ),
        out_specs=(P(None, "dp", "tensor"), P(("tensor", "dp"), None), P(("tensor", "dp"), None)),
        check_vma=False,
    )
```

```python
import functools

import jax
import jax.numpy as jnp
from jax import lax
from jax.experimental import pallas as pl
from jax.experimental.pallas import tpu as pltpu
from jax.sharding import PartitionSpec as P

MESH = pl.DeviceIdType.MESH
corr_one = 1.0 - 0.9**10
corr_two = 1.0 - 0.999**10

HEAD = 80
SLABS = 2
NZ, NX, NC, NY = 8, 4, 2, 4
bf16, f32 = jnp.bfloat16, jnp.float32


def adam(grad, first, second):
    new_first = 0.9 * first + 0.1 * grad
    new_second = 0.999 * second + 0.001 * grad * grad
    return new_first, new_second


def normalize(new_first, new_second):
    return new_first / corr_one / (jnp.sqrt(new_second / corr_two) + 1e-08)


def reduce_gather(
    tokens, acts, proj, grads, first, second,
    update, new_first, new_second,
    acts_v, proj_v, rows_v, grads_v, first_v, second_v,
    xp_own, xp_in, part, part_send, core_in, x_send, x_in, z_send, z_in, tail_zin, tail_own, tail_send, tail_xin, gathered,
    in_sem, slab_sem, og_sem, y_s, y_r, c_s, c_r, x_s, x_r, z_s, z_r,
    gz_s, gz_r, gx_s, gx_r, gc_s, gc_r,
    tz_s, tz_r, tx_s, tx_r, gtz_s, gtz_r, gtx_s, gtx_r,
):
    t_count, _, columns = grads.shape
    group = columns // NZ
    own = group // (NX * NC)
    width = acts.shape[1]
    rank = proj.shape[1]
    pair = 2 * rank
    dp, y = lax.axis_index("dp"), lax.axis_index("tensor")
    z, x, c = dp // (NX * NC), lax.rem(dp // NC, NX), lax.rem(dp, NC)

    def zdev(j):
        return ((lax.rem(z + j, NZ) * NX + x) * NC + c, y)

    def xdev(j):
        return ((z * NX + lax.rem(x + j, NX)) * NC + c, y)

    def ydev(j):
        return (dp, lax.rem(y + j, NY))

    head, tail = pl.ds(0, HEAD), pl.ds(HEAD, own - HEAD)
    sibling = ((z * NX + x) * NC + (1 - c), y)

    def remote(src, dst, s, r, device):
        return pltpu.make_async_remote_copy(
            src_ref=src, dst_ref=dst, send_sem=s, recv_sem=r, device_id=device, device_id_type=MESH
        )

    slab = width // SLABS

    def load_slab(i):
        span = pl.ds(i * slab, slab)
        there = pl.ds(pl.multiple_of(y * width + i * slab, 128), slab)
        return (
            pltpu.make_async_copy(acts.at[:, span], acts_v.at[:, span], slab_sem.at[0, i]),
            pltpu.make_async_copy(proj.at[:, :, there], proj_v.at[:, :, span], slab_sem.at[1, i]),
        )

    load_first = pltpu.make_async_copy(first, first_v, in_sem.at[2])
    load_second = pltpu.make_async_copy(second, second_v, in_sem.at[3])
    rows = update.shape[1]
    load_rows = pltpu.make_async_copy(proj.at[:, :, pl.ds(pl.multiple_of(dp * rows, 128), rows)], rows_v, in_sem.at[4])
    for i in range(SLABS):
        for load in load_slab(i):
            load.start()
    load_rows.start()

    def offset(s):
        return NZ // 2 + (1 - 2 * lax.rem(s, 2)) * ((s + 1) // 2)

    def load_group(s):
        g = lax.rem(z + offset(s), NZ)
        span = pl.ds(pl.multiple_of(g * group, 128), group)
        return pltpu.make_async_copy(grads.at[:, :, span], grads_v.at[s], og_sem.at[s])

    barrier = pltpu.get_barrier_semaphore()
    peers = [zdev(j) for j in range(1, NZ)] + [xdev(j) for j in range(1, NX)] + [ydev(j) for j in range(1, NY)] + [sibling]
    for peer in peers:
        pl.semaphore_signal(barrier, inc=1, device_id=peer, device_id_type=MESH)

    nt = (((1,), (1,)), ((), ()))
    xp = None
    for i in range(SLABS):
        for load in load_slab(i):
            load.wait()
        span = pl.ds(i * slab, slab)
        term = lax.dot_general(acts_v[:, span], proj_v[:, :, span].reshape(pair, slab), nt, preferred_element_type=f32)
        xp = term if i == 0 else xp + term
    xp_own[...] = xp.astype(bf16)
    pl.semaphore_wait(barrier, len(peers))

    @pl.loop(0, NZ)
    def _(s):
        load_group(s).start()

    load_first.start()
    load_second.start()

    y_copies = [remote(xp_own, xp_in.at[j - 1], y_s.at[j - 1], y_r.at[j - 1], ydev(j)) for j in range(1, NY)]
    for j in (1, 0, 2):
        y_copies[j].start()
    row = lax.broadcasted_iota(jnp.int32, (t_count, 2 * t_count), 0)
    col = lax.broadcasted_iota(jnp.int32, (t_count, 2 * t_count), 1)
    spread = jnp.where(row == col // 2, 1.0, 0.0).astype(bf16)
    load_rows.wait()
    flat = rows_v[...].reshape(pair, rows)
    flat = jnp.concatenate([flat, flat], axis=1)
    row = lax.broadcasted_iota(jnp.int32, flat.shape, 0)
    col = lax.broadcasted_iota(jnp.int32, flat.shape, 1)
    decoder = jnp.where(row // rank == col // rows, flat.astype(f32), 0.0).T.astype(bf16)
    for copy in y_copies:
        copy.wait_recv()
    reduced = (xp + xp_in[0].astype(f32) + xp_in[1].astype(f32) + xp_in[2].astype(f32)).astype(bf16)
    weights = jnp.dot(reduced.T, spread, preferred_element_type=f32)
    row = lax.broadcasted_iota(jnp.int32, (pair, 2 * t_count), 0)
    col = lax.broadcasted_iota(jnp.int32, (pair, 2 * t_count), 1)
    weights = jnp.where(lax.rem(col, 2) == row // rank, weights, 0.0).astype(bf16)

    def core_copy(s):
        return remote(part_send.at[s, :, 1 - c], core_in.at[s], c_s.at[s], c_r.at[s], sibling)

    def x_copy(s, j):
        return remote(x_send.at[s, lax.rem(x + j, NX), head], x_in.at[s, j - 1], x_s.at[s, j - 1], x_r.at[s, j - 1], xdev(j))

    def z_copy(s):
        j = offset(s)
        return remote(z_send.at[s], z_in.at[s], z_s.at[s], z_r.at[s], zdev(j))

    def tz_copy(s):
        return remote(x_send.at[s, :, tail], tail_zin.at[s], tz_s.at[s], tz_r.at[s], zdev(offset(s)))

    def tx_copy(j):
        return remote(tail_send.at[lax.rem(x + j, NX)], tail_xin.at[j - 1], tx_s.at[j - 1], tx_r.at[j - 1], xdev(j))

    lag = 3

    @pl.loop(0, NZ + lag)
    def _(step):
        @pl.when(step < NZ)
        def _():
            load_group(step).wait()
            block = grads_v[step].reshape(2 * t_count, group)
            terms = jnp.dot(weights, block, preferred_element_type=f32).T.reshape(NX, NC, own, pair)
            part_send[step] = terms.astype(bf16)
            core_copy(step).start()
            part[step] = terms

        @pl.when(step >= lag)
        def _():
            s = step - lag
            core_copy(s).wait_recv()
            x_send[s] = (part[s, :, c] + core_in[s].astype(f32)).astype(bf16)
            for j in (2, 1, 3):
                x_copy(s, j).start()

            @pl.when(s < NZ - 1)
            def _():
                tz_copy(s).start()

    def x_sum(s):
        for j in range(1, NX):
            x_copy(s, j).wait_recv()
        total = part[s, x, c, head] + core_in[s, x, head].astype(f32)
        for j in range(NX - 1):
            total += x_in[s, j].astype(f32)
        return total

    def x_then_z(s):
        z_send[s] = x_sum(s).astype(bf16)
        z_copy(s).start()

    pl.loop(0, 4)(x_then_z)
    tails = part[NZ - 1, :, c, tail] + core_in[NZ - 1, :, tail].astype(f32)
    for s in range(NZ - 1):
        tz_copy(s).wait_recv()
        tails += tail_zin[s].astype(f32)
    tail_send[...] = tails.astype(bf16)
    tail_own[...] = tails
    for j in (2, 1, 3):
        tx_copy(j).start()
    pl.loop(4, NZ - 1)(x_then_z)

    load_first.wait()
    load_second.wait()

    def finish(span, total):
        grad = total / f32(tokens)
        new_first[span], new_second[span] = adam(grad, first_v[span], second_v[span])
        gathered[z, x, c, span] = normalize(new_first[span], new_second[span]).astype(bf16)

    total = tail_own[x]
    for j in range(1, NX):
        tx_copy(j).wait_recv()
        total += tail_xin[j - 1].astype(f32)
    finish(tail, total)
    total = x_sum(NZ - 1)
    for s in range(NZ - 1):
        z_copy(s).wait_recv()
        total += z_in[s].astype(f32)
    finish(head, total)

    def gz_copy(j):
        here = gathered.at[z, x, c, head]
        return remote(here, here, gz_s.at[j - 1], gz_r.at[j - 1], zdev(j))

    def gz_arrival(j):
        here = gathered.at[lax.rem(z + NZ - j, NZ), x, c, head]
        return remote(here, here, gz_s.at[j - 1], gz_r.at[j - 1], zdev(j))

    def near(s):
        return offset(NZ - 1 - s)

    def gx_copy(s, j):
        here = gathered.at[lax.rem(z + NZ - near(s), NZ), x, c, head]
        return remote(here, here, gx_s.at[s, j - 1], gx_r.at[s, j - 1], xdev(j))

    def gx_arrival(s, j):
        here = gathered.at[lax.rem(z + NZ - near(s), NZ), lax.rem(x + NX - j, NX), c, head]
        return remote(here, here, gx_s.at[s, j - 1], gx_r.at[s, j - 1], xdev(j))

    def gtx_copy(j):
        here = gathered.at[z, x, c, tail]
        return remote(here, here, gtx_s.at[j - 1], gtx_r.at[j - 1], xdev(j))

    def gtx_arrival(j):
        here = gathered.at[z, lax.rem(x + NX - j, NX), c, tail]
        return remote(here, here, gtx_s.at[j - 1], gtx_r.at[j - 1], xdev(j))

    def gtz_copy(j):
        here = gathered.at[z, :, c, tail]
        return remote(here, here, gtz_s.at[j - 1], gtz_r.at[j - 1], zdev(j))

    def gtz_arrival(j):
        here = gathered.at[lax.rem(z + NZ - j, NZ), :, c, tail]
        return remote(here, here, gtz_s.at[j - 1], gtz_r.at[j - 1], zdev(j))

    def gc_copy(s):
        here = gathered.at[lax.rem(z + NZ - near(s), NZ), :, c]
        return remote(here, here, gc_s.at[s], gc_r.at[s], sibling)

    def gc_arrival(s):
        here = gathered.at[lax.rem(z + NZ - near(s), NZ), :, 1 - c]
        return remote(here, here, gc_s.at[s], gc_r.at[s], sibling)

    for j in (2, 1, 3):
        gtx_copy(j).start()
    for j in (1, 7, 2, 6, 3, 5, 4):
        gz_copy(j).start()

    x_lag, core_lag = 7, 10

    @pl.loop(0, NZ + core_lag)
    def _(step):
        @pl.when(step < NZ)
        def _():
            @pl.when(step > 0)
            def _():
                gz_arrival(near(step)).wait_recv()

            for j in (2, 1, 3):
                gx_copy(step, j).start()

            core_copy(step).wait_send()
            for j in range(1, NX):
                x_copy(step, j).wait_send()

            @pl.when(step < NZ - 1)
            def _():
                z_copy(step).wait_send()
                tz_copy(step).wait_send()

        @pl.when(step == 1)
        def _():
            for j in range(1, NX):
                gtx_arrival(j).wait_recv()
            for j in (1, 7, 2, 6, 3, 5, 4):
                gtz_copy(j).start()
            for j in range(1, NX):
                y_copies[j - 1].wait_send()
                tx_copy(j).wait_send()
                gtx_copy(j).wait_send()

        @pl.when((step >= x_lag) & (step < NZ + x_lag))
        def _():
            s = step - x_lag
            for j in range(1, NX):
                gx_arrival(s, j).wait_recv()

            @pl.when(s > 0)
            def _():
                gtz_arrival(near(s)).wait_recv()

            gc_copy(s).start()

        @pl.when(step >= core_lag)
        def _():
            s = step - core_lag
            gc_arrival(s).wait_recv()
            g = lax.rem(z + NZ - near(s), NZ)
            block = gathered[g].reshape(group, pair)
            out = lax.dot_general(decoder, block, nt, preferred_element_type=f32)
            update[:, :, pl.ds(pl.multiple_of(g * group, 128), group)] = out.astype(bf16).reshape(2, rows, group)
            gc_copy(s).wait_send()
            for j in range(1, NX):
                gx_copy(s, j).wait_send()

    for j in range(1, NZ):
        gz_copy(j).wait_send()
        gtz_copy(j).wait_send()


def publish(update, first, second, update_out, first_out, second_out, sem):
    pieces = update.shape[1] // 4
    copies = [
        pltpu.make_async_copy(update.at[:, pl.ds(i * pieces, pieces)], update_out.at[:, pl.ds(i * pieces, pieces)], sem.at[i])
        for i in range(4)
    ]
    copies.append(pltpu.make_async_copy(first, first_out, sem.at[4]))
    copies.append(pltpu.make_async_copy(second, second_out, sem.at[5]))
    for copy in copies:
        copy.start()
    for copy in copies:
        copy.wait()


def local(acts, out_grads, projectors, moment_first, moment_second):
    t_count, width = acts.shape
    columns = out_grads.shape[2]
    rank = projectors.shape[2]
    pair = 2 * rank
    dp_count = lax.axis_size("dp")
    own = columns // dp_count
    group = columns // NZ
    proj = jnp.swapaxes(projectors, 1, 2)
    rows = projectors.shape[1] // dp_count
    inputs = [pltpu.with_memory_space_constraint(a, pltpu.HBM) for a in (acts, proj, out_grads, moment_first, moment_second)]
    hbm = pl.BlockSpec(memory_space=pltpu.HBM)
    vmem = pl.BlockSpec(memory_space=pltpu.VMEM)
    dma = pltpu.SemaphoreType.DMA
    results = pl.pallas_call(
        functools.partial(reduce_gather, t_count * dp_count),
        out_shape=(
            pltpu.VMEM((2, rows, columns), bf16),
            pltpu.VMEM((own, pair), f32),
            pltpu.VMEM((own, pair), f32),
        ),
        in_specs=[hbm] * 5,
        out_specs=(vmem, vmem, vmem),
        scratch_shapes=[
            pltpu.VMEM((t_count, width), bf16),
            pltpu.VMEM((2, rank, width), bf16),
            pltpu.VMEM((2, rank, rows), bf16),
            pltpu.VMEM((NZ, t_count, 2, group), bf16),
            pltpu.VMEM((own, pair), f32),
            pltpu.VMEM((own, pair), f32),
            pltpu.VMEM((t_count, pair), bf16),
            pltpu.VMEM((NY - 1, t_count, pair), bf16),
            pltpu.VMEM((NZ, NX, NC, own, pair), f32),
            pltpu.VMEM((NZ, NX, NC, own, pair), bf16),
            pltpu.VMEM((NZ, NX, own, pair), bf16),
            pltpu.VMEM((NZ, NX, own, pair), bf16),
            pltpu.VMEM((NZ, NX - 1, HEAD, pair), bf16),
            pltpu.VMEM((NZ - 1, HEAD, pair), bf16),
            pltpu.VMEM((NZ - 1, HEAD, pair), bf16),
            pltpu.VMEM((NZ - 1, NX, own - HEAD, pair), bf16),
            pltpu.VMEM((NX, own - HEAD, pair), f32),
            pltpu.VMEM((NX, own - HEAD, pair), bf16),
            pltpu.VMEM((NX - 1, own - HEAD, pair), bf16),
            pltpu.VMEM((NZ, NX, NC, own, pair), bf16),
            dma((5,)),
            dma((2, SLABS)),
            dma((NZ,)),
            dma((NY - 1,)),
            dma((NY - 1,)),
            dma((NZ,)),
            dma((NZ,)),
            dma((NZ, NX - 1)),
            dma((NZ, NX - 1)),
            dma((NZ - 1,)),
            dma((NZ - 1,)),
            dma((NZ - 1,)),
            dma((NZ - 1,)),
            dma((NZ, NX - 1)),
            dma((NZ, NX - 1)),
            dma((NZ,)),
            dma((NZ,)),
            dma((NZ - 1,)),
            dma((NZ - 1,)),
            dma((NX - 1,)),
            dma((NX - 1,)),
            dma((NZ - 1,)),
            dma((NZ - 1,)),
            dma((NX - 1,)),
            dma((NX - 1,)),
        ],
        compiler_params=pltpu.CompilerParams(collective_id=0, has_side_effects=True, vmem_limit_bytes=40 << 20),
        name="rank_adam",
    )(*inputs)
    return pl.pallas_call(
        publish,
        out_shape=tuple(jax.ShapeDtypeStruct(r.shape, r.dtype) for r in results),
        in_specs=[vmem] * 3,
        out_specs=[hbm] * 3,
        scratch_shapes=[dma((6,))],
        compiler_params=pltpu.CompilerParams(vmem_limit_bytes=4 << 20),
        name="publish",
    )(*[pltpu.with_memory_space_constraint(r, pltpu.VMEM) for r in results])


def solution(mesh):
    return jax.shard_map(
        local,
        mesh=mesh,
        in_specs=(
            P("dp", "tensor"),
            P("dp", None, "tensor"),
            P(),
            P(("tensor", "dp"), None),
            P(("tensor", "dp"), None),
        ),
        out_specs=(P(None, "dp", "tensor"), P(("tensor", "dp"), None), P(("tensor", "dp"), None)),
        check_vma=False,
    )
```

```python
import functools

import jax
import jax.numpy as jnp
from jax import lax
from jax.experimental import pallas as pl
from jax.experimental.pallas import tpu as pltpu
from jax.sharding import PartitionSpec as P

MESH = pl.DeviceIdType.MESH
corr_one = 1.0 - 0.9**10
corr_two = 1.0 - 0.999**10

HEAD = 80
SLABS = 2
NZ, NX, NC, NY = 8, 4, 2, 4
bf16, f32 = jnp.bfloat16, jnp.float32


def adam(grad, first, second):
    new_first = 0.9 * first + 0.1 * grad
    new_second = 0.999 * second + 0.001 * grad * grad
    return new_first, new_second


def normalize(new_first, new_second):
    return new_first / corr_one / (jnp.sqrt(new_second / corr_two) + 1e-08)


def reduce_gather(
    tokens, acts, proj, grads, first, second,
    update, new_first, new_second,
    acts_v, proj_v, rows_v, grads_v, first_v, second_v,
    xp_own, xp_in, part, part_send, core_in, x_send, x_in, z_send, z_in, tail_zin, tail_own, tail_send, tail_xin, gathered,
    in_sem, slab_sem, og_sem, y_s, y_r, c_s, c_r, x_s, x_r, z_s, z_r,
    gz_s, gz_r, gx_s, gx_r, gc_s, gc_r,
    tz_s, tz_r, tx_s, tx_r, gtz_s, gtz_r, gtx_s, gtx_r,
):
    t_count, _, columns = grads.shape
    group = columns // NZ
    own = group // (NX * NC)
    width = acts.shape[1]
    rank = proj.shape[1]
    pair = 2 * rank
    dp, y = lax.axis_index("dp"), lax.axis_index("tensor")
    z, x, c = dp // (NX * NC), lax.rem(dp // NC, NX), lax.rem(dp, NC)

    def zdev(j):
        return ((lax.rem(z + j, NZ) * NX + x) * NC + c, y)

    def xdev(j):
        return ((z * NX + lax.rem(x + j, NX)) * NC + c, y)

    def ydev(j):
        return (dp, lax.rem(y + j, NY))

    head, tail = pl.ds(0, HEAD), pl.ds(HEAD, own - HEAD)
    sibling = ((z * NX + x) * NC + (1 - c), y)

    def remote(src, dst, s, r, device):
        return pltpu.make_async_remote_copy(
            src_ref=src, dst_ref=dst, send_sem=s, recv_sem=r, device_id=device, device_id_type=MESH
        )

    slab = width // SLABS

    def load_slab(i):
        span = pl.ds(i * slab, slab)
        there = pl.ds(pl.multiple_of(y * width + i * slab, 128), slab)
        return (
            pltpu.make_async_copy(acts.at[:, span], acts_v.at[:, span], slab_sem.at[0, i]),
            pltpu.make_async_copy(proj.at[:, :, there], proj_v.at[:, :, span], slab_sem.at[1, i]),
        )

    load_first = pltpu.make_async_copy(first, first_v, in_sem.at[2])
    load_second = pltpu.make_async_copy(second, second_v, in_sem.at[3])
    rows = update.shape[1]
    load_rows = pltpu.make_async_copy(proj.at[:, :, pl.ds(pl.multiple_of(dp * rows, 128), rows)], rows_v, in_sem.at[4])
    for i in range(SLABS):
        for load in load_slab(i):
            load.start()
    load_rows.start()

    def offset(s):
        return NZ // 2 + (1 - 2 * lax.rem(s, 2)) * ((s + 1) // 2)

    def load_group(s):
        g = lax.rem(z + offset(s), NZ)
        span = pl.ds(pl.multiple_of(g * group, 128), group)
        return pltpu.make_async_copy(grads.at[:, :, span], grads_v.at[s], og_sem.at[s])

    barrier = pltpu.get_barrier_semaphore()
    peers = [zdev(j) for j in range(1, NZ)] + [xdev(j) for j in range(1, NX)] + [ydev(j) for j in range(1, NY)] + [sibling]
    for peer in peers:
        pl.semaphore_signal(barrier, inc=1, device_id=peer, device_id_type=MESH)

    nt = (((1,), (1,)), ((), ()))
    xp = None
    for i in range(SLABS):
        for load in load_slab(i):
            load.wait()
        span = pl.ds(i * slab, slab)
        term = lax.dot_general(acts_v[:, span], proj_v[:, :, span].reshape(pair, slab), nt, preferred_element_type=f32)
        xp = term if i == 0 else xp + term
    xp_own[...] = xp.astype(bf16)
    pl.semaphore_wait(barrier, len(peers))

    @pl.loop(0, NZ)
    def _(s):
        load_group(s).start()

    load_first.start()
    load_second.start()

    y_copies = [remote(xp_own, xp_in.at[j - 1], y_s.at[j - 1], y_r.at[j - 1], ydev(j)) for j in range(1, NY)]
    for j in (1, 0, 2):
        y_copies[j].start()
    row = lax.broadcasted_iota(jnp.int32, (t_count, 2 * t_count), 0)
    col = lax.broadcasted_iota(jnp.int32, (t_count, 2 * t_count), 1)
    spread = jnp.where(row == col // 2, 1.0, 0.0).astype(bf16)
    load_rows.wait()
    flat = rows_v[...].reshape(pair, rows)
    flat = jnp.concatenate([flat, flat], axis=1)
    row = lax.broadcasted_iota(jnp.int32, flat.shape, 0)
    col = lax.broadcasted_iota(jnp.int32, flat.shape, 1)
    decoder = jnp.where(row // rank == col // rows, flat.astype(f32), 0.0).T.astype(bf16)
    for copy in y_copies:
        copy.wait_recv()
    reduced = (xp + xp_in[0].astype(f32) + xp_in[1].astype(f32) + xp_in[2].astype(f32)).astype(bf16)
    weights = jnp.dot(reduced.T, spread, preferred_element_type=f32)
    row = lax.broadcasted_iota(jnp.int32, (pair, 2 * t_count), 0)
    col = lax.broadcasted_iota(jnp.int32, (pair, 2 * t_count), 1)
    weights = jnp.where(lax.rem(col, 2) == row // rank, weights, 0.0).astype(bf16)

    def core_copy(s):
        return remote(part_send.at[s, :, 1 - c], core_in.at[s], c_s.at[s], c_r.at[s], sibling)

    def x_copy(s, j):
        return remote(x_send.at[s, lax.rem(x + j, NX), head], x_in.at[s, j - 1], x_s.at[s, j - 1], x_r.at[s, j - 1], xdev(j))

    def z_copy(s):
        j = offset(s)
        return remote(z_send.at[s], z_in.at[s], z_s.at[s], z_r.at[s], zdev(j))

    def tz_copy(s):
        return remote(x_send.at[s, :, tail], tail_zin.at[s], tz_s.at[s], tz_r.at[s], zdev(offset(s)))

    def tx_copy(j):
        return remote(tail_send.at[lax.rem(x + j, NX)], tail_xin.at[j - 1], tx_s.at[j - 1], tx_r.at[j - 1], xdev(j))

    lag = 3

    @pl.loop(0, NZ + lag)
    def _(step):
        @pl.when(step < NZ)
        def _():
            load_group(step).wait()
            block = grads_v[step].reshape(2 * t_count, group)
            terms = jnp.dot(weights, block, preferred_element_type=f32).T.reshape(NX, NC, own, pair)
            part_send[step] = terms.astype(bf16)
            core_copy(step).start()
            part[step] = terms

        @pl.when(step >= lag)
        def _():
            s = step - lag
            core_copy(s).wait_recv()
            x_send[s] = (part[s, :, c] + core_in[s].astype(f32)).astype(bf16)
            for j in (2, 1, 3):
                x_copy(s, j).start()

            @pl.when(s < NZ - 1)
            def _():
                tz_copy(s).start()

    def x_sum(s):
        for j in range(1, NX):
            x_copy(s, j).wait_recv()
        total = part[s, x, c, head] + core_in[s, x, head].astype(f32)
        for j in range(NX - 1):
            total += x_in[s, j].astype(f32)
        return total

    def x_then_z(s):
        z_send[s] = x_sum(s).astype(bf16)
        z_copy(s).start()

    pl.loop(0, 4)(x_then_z)
    tails = part[NZ - 1, :, c, tail] + core_in[NZ - 1, :, tail].astype(f32)
    for s in range(NZ - 1):
        tz_copy(s).wait_recv()
        tails += tail_zin[s].astype(f32)
    tail_send[...] = tails.astype(bf16)
    tail_own[...] = tails
    for j in (2, 1, 3):
        tx_copy(j).start()
    pl.loop(4, NZ - 1)(x_then_z)

    load_first.wait()
    load_second.wait()

    def finish(span, total):
        grad = total / f32(tokens)
        new_first[span], new_second[span] = adam(grad, first_v[span], second_v[span])
        gathered[z, x, c, span] = normalize(new_first[span], new_second[span]).astype(bf16)

    total = tail_own[x]
    for j in range(1, NX):
        tx_copy(j).wait_recv()
        total += tail_xin[j - 1].astype(f32)
    finish(tail, total)
    total = x_sum(NZ - 1)
    for s in range(NZ - 1):
        z_copy(s).wait_recv()
        total += z_in[s].astype(f32)
    finish(head, total)

    def gz_copy(j):
        here = gathered.at[z, x, c, head]
        return remote(here, here, gz_s.at[j - 1], gz_r.at[j - 1], zdev(j))

    def gz_arrival(j):
        here = gathered.at[lax.rem(z + NZ - j, NZ), x, c, head]
        return remote(here, here, gz_s.at[j - 1], gz_r.at[j - 1], zdev(j))

    def near(s):
        return offset(NZ - 1 - s)

    def gx_copy(s, j):
        here = gathered.at[lax.rem(z + NZ - near(s), NZ), x, c, head]
        return remote(here, here, gx_s.at[s, j - 1], gx_r.at[s, j - 1], xdev(j))

    def gx_arrival(s, j):
        here = gathered.at[lax.rem(z + NZ - near(s), NZ), lax.rem(x + NX - j, NX), c, head]
        return remote(here, here, gx_s.at[s, j - 1], gx_r.at[s, j - 1], xdev(j))

    def gtx_copy(j):
        here = gathered.at[z, x, c, tail]
        return remote(here, here, gtx_s.at[j - 1], gtx_r.at[j - 1], xdev(j))

    def gtx_arrival(j):
        here = gathered.at[z, lax.rem(x + NX - j, NX), c, tail]
        return remote(here, here, gtx_s.at[j - 1], gtx_r.at[j - 1], xdev(j))

    def gtz_copy(j):
        here = gathered.at[z, :, c, tail]
        return remote(here, here, gtz_s.at[j - 1], gtz_r.at[j - 1], zdev(j))

    def gtz_arrival(j):
        here = gathered.at[lax.rem(z + NZ - j, NZ), :, c, tail]
        return remote(here, here, gtz_s.at[j - 1], gtz_r.at[j - 1], zdev(j))

    def gc_copy(s):
        here = gathered.at[lax.rem(z + NZ - near(s), NZ), :, c]
        return remote(here, here, gc_s.at[s], gc_r.at[s], sibling)

    def gc_arrival(s):
        here = gathered.at[lax.rem(z + NZ - near(s), NZ), :, 1 - c]
        return remote(here, here, gc_s.at[s], gc_r.at[s], sibling)

    for j in (2, 1, 3):
        gtx_copy(j).start()
    for j in (1, 7, 2, 6, 3, 5, 4):
        gz_copy(j).start()

    x_lag, core_lag = 7, 10

    @pl.loop(0, NZ + core_lag)
    def _(step):
        @pl.when(step < NZ)
        def _():
            @pl.when(step > 0)
            def _():
                gz_arrival(near(step)).wait_recv()

            for j in (2, 1, 3):
                gx_copy(step, j).start()

            core_copy(step).wait_send()
            for j in range(1, NX):
                x_copy(step, j).wait_send()

            @pl.when(step < NZ - 1)
            def _():
                z_copy(step).wait_send()
                tz_copy(step).wait_send()

        @pl.when(step == 1)
        def _():
            for j in range(1, NX):
                gtx_arrival(j).wait_recv()
            for j in (4, 3, 5, 2, 6, 1, 7):
                gtz_copy(j).start()
            for j in range(1, NX):
                y_copies[j - 1].wait_send()
                tx_copy(j).wait_send()
                gtx_copy(j).wait_send()

        @pl.when((step >= x_lag) & (step < NZ + x_lag))
        def _():
            s = step - x_lag
            for j in range(1, NX):
                gx_arrival(s, j).wait_recv()

            @pl.when(s > 0)
            def _():
                gtz_arrival(near(s)).wait_recv()

            gc_copy(s).start()

        @pl.when(step >= core_lag)
        def _():
            s = step - core_lag
            gc_arrival(s).wait_recv()
            g = lax.rem(z + NZ - near(s), NZ)
            block = gathered[g].reshape(group, pair)
            out = lax.dot_general(decoder, block, nt, preferred_element_type=f32)
            update[:, :, pl.ds(pl.multiple_of(g * group, 128), group)] = out.astype(bf16).reshape(2, rows, group)
            gc_copy(s).wait_send()
            for j in range(1, NX):
                gx_copy(s, j).wait_send()

    for j in range(1, NZ):
        gz_copy(j).wait_send()
        gtz_copy(j).wait_send()


def publish(update, first, second, update_out, first_out, second_out, sem):
    pieces = update.shape[1] // 4
    copies = [
        pltpu.make_async_copy(update.at[:, pl.ds(i * pieces, pieces)], update_out.at[:, pl.ds(i * pieces, pieces)], sem.at[i])
        for i in range(4)
    ]
    copies.append(pltpu.make_async_copy(first, first_out, sem.at[4]))
    copies.append(pltpu.make_async_copy(second, second_out, sem.at[5]))
    for copy in copies:
        copy.start()
    for copy in copies:
        copy.wait()


def local(acts, out_grads, projectors, moment_first, moment_second):
    t_count, width = acts.shape
    columns = out_grads.shape[2]
    rank = projectors.shape[2]
    pair = 2 * rank
    dp_count = lax.axis_size("dp")
    own = columns // dp_count
    group = columns // NZ
    proj = jnp.swapaxes(projectors, 1, 2)
    rows = projectors.shape[1] // dp_count
    inputs = [pltpu.with_memory_space_constraint(a, pltpu.HBM) for a in (acts, proj, out_grads, moment_first, moment_second)]
    hbm = pl.BlockSpec(memory_space=pltpu.HBM)
    vmem = pl.BlockSpec(memory_space=pltpu.VMEM)
    dma = pltpu.SemaphoreType.DMA
    results = pl.pallas_call(
        functools.partial(reduce_gather, t_count * dp_count),
        out_shape=(
            pltpu.VMEM((2, rows, columns), bf16),
            pltpu.VMEM((own, pair), f32),
            pltpu.VMEM((own, pair), f32),
        ),
        in_specs=[hbm] * 5,
        out_specs=(vmem, vmem, vmem),
        scratch_shapes=[
            pltpu.VMEM((t_count, width), bf16),
            pltpu.VMEM((2, rank, width), bf16),
            pltpu.VMEM((2, rank, rows), bf16),
            pltpu.VMEM((NZ, t_count, 2, group), bf16),
            pltpu.VMEM((own, pair), f32),
            pltpu.VMEM((own, pair), f32),
            pltpu.VMEM((t_count, pair), bf16),
            pltpu.VMEM((NY - 1, t_count, pair), bf16),
            pltpu.VMEM((NZ, NX, NC, own, pair), f32),
            pltpu.VMEM((NZ, NX, NC, own, pair), bf16),
            pltpu.VMEM((NZ, NX, own, pair), bf16),
            pltpu.VMEM((NZ, NX, own, pair), bf16),
            pltpu.VMEM((NZ, NX - 1, HEAD, pair), bf16),
            pltpu.VMEM((NZ - 1, HEAD, pair), bf16),
            pltpu.VMEM((NZ - 1, HEAD, pair), bf16),
            pltpu.VMEM((NZ - 1, NX, own - HEAD, pair), bf16),
            pltpu.VMEM((NX, own - HEAD, pair), f32),
            pltpu.VMEM((NX, own - HEAD, pair), bf16),
            pltpu.VMEM((NX - 1, own - HEAD, pair), bf16),
            pltpu.VMEM((NZ, NX, NC, own, pair), bf16),
            dma((5,)),
            dma((2, SLABS)),
            dma((NZ,)),
            dma((NY - 1,)),
            dma((NY - 1,)),
            dma((NZ,)),
            dma((NZ,)),
            dma((NZ, NX - 1)),
            dma((NZ, NX - 1)),
            dma((NZ - 1,)),
            dma((NZ - 1,)),
            dma((NZ - 1,)),
            dma((NZ - 1,)),
            dma((NZ, NX - 1)),
            dma((NZ, NX - 1)),
            dma((NZ,)),
            dma((NZ,)),
            dma((NZ - 1,)),
            dma((NZ - 1,)),
            dma((NX - 1,)),
            dma((NX - 1,)),
            dma((NZ - 1,)),
            dma((NZ - 1,)),
            dma((NX - 1,)),
            dma((NX - 1,)),
        ],
        compiler_params=pltpu.CompilerParams(collective_id=0, has_side_effects=True, vmem_limit_bytes=40 << 20),
        name="rank_adam",
    )(*inputs)
    return pl.pallas_call(
        publish,
        out_shape=tuple(jax.ShapeDtypeStruct(r.shape, r.dtype) for r in results),
        in_specs=[vmem] * 3,
        out_specs=[hbm] * 3,
        scratch_shapes=[dma((6,))],
        compiler_params=pltpu.CompilerParams(vmem_limit_bytes=4 << 20),
        name="publish",
    )(*[pltpu.with_memory_space_constraint(r, pltpu.VMEM) for r in results])


def solution(mesh):
    return jax.shard_map(
        local,
        mesh=mesh,
        in_specs=(
            P("dp", "tensor"),
            P("dp", None, "tensor"),
            P(),
            P(("tensor", "dp"), None),
            P(("tensor", "dp"), None),
        ),
        out_specs=(P(None, "dp", "tensor"), P(("tensor", "dp"), None), P(("tensor", "dp"), None)),
        check_vma=False,
    )
```
